32 devices in a mesh: copies: 2 (over y), blk: 4 (over x, core), rows: 4 (over z).
Axes of the slice: x: 2, y: 2, z: 4, core: 2. Of those that a mesh axis runs over, the one named last changes fastest.
Arguments:
- activations: bfloat16 [3584, 4096], P(('copies', 'blk'), 'rows'), parts along dimension 0, may hold values from -6 to 6
- out_grads: bfloat16 [3584, 14848], P(('copies', 'blk'), 'rows'), parts along dimension 0, may hold values from -6 to 6
- eigvecs: float32 [4, 4096, 14848], P('blk', 'rows'), may hold values from -0.0007324219 to 0.0007324219
- eigvals: float32 [4], replicated, may hold values from 0.5 to 4
- segment_ids: int32 [3584], P(('copies', 'blk')), parts along dimension 0, may hold values from 0 to 111, never falling along the last dimension, each value on 1 to 64 neighbouring positions
Outputs:
- influence: float32 [224, 4], P('copies'), parts along dimension 0
The draws below stay inside these ranges and needn't reach their ends.
There are 2 independent parts, one for each index of `copies`. The reference program is written for one: setup_inputs(seed, part) draws one part's arguments, and reference() takes and returns one part's arrays. A program takes and returns all parts, laid end to end along the dimension named above; an argument that names none is the same for every part. Nothing has to cross between parts.
Inputs may be any that keep to these rules, and one draw needn't show every extreme that they name: `segment_ids`: never falling along the tokens; each example holds 1 to 64 consecutive tokens, one exactly 64; examples may cross from one index of blk to the next.
All inputs are finite; a program needn't handle non-finite values.
Results may differ from the reference program's by a relative error of at most 0.0029.
Values may be sent and summed in bfloat16 or wider, within the bound.
A program may use at most 384 MiB of HBM per device.

```python
import math
import jax
import jax.numpy as jnp
import numpy as np
from jax import lax

D = 4096
F = 14848
TOK_DEV = 448
SEG_MEAN = 16
SEG_MOST = 64
EIGS = 4
TOKENS = 1792
EXAMPLES = 112
N_BLK = 4


def steps_of(rng, shape, pieces, low, high):
    factor_of, own = 1.0, jax.random.fold_in(rng, 6)
    for dim, shards_of in pieces:
        heights = jnp.exp(jax.random.uniform(jax.random.fold_in(own, dim), (shards_of,), jnp.float32, low / len(pieces), high / len(pieces)))
        factor_of = factor_of * jnp.repeat(heights, shape[dim] // shards_of).reshape([-1 if axis == dim else 1 for axis in range(len(shape))])
    return factor_of


def length_profile(amount, total, bound, slope):
    portions = [(1 << 20) // math.isqrt(standing ** slope) + 1 for standing in range(2, amount + 1)]
    spare, counts = total - bound - (amount - 1), [1] * (amount - 1)
    while spare > 0:
        free = [i for i in range(amount - 1) if counts[i] < bound]
        mass, remaining = sum([portions[i] for i in free]), spare
        for i in free:
            addition = min(bound - counts[i], max(1, remaining * portions[i] // mass), spare)
            counts[i] = counts[i] + addition
            spare = spare - addition
    return np.array([bound] + counts)


def ragged_sizes(own_key, number_of, total, bound, lean):
    if number_of == 2:
        one = jax.random.randint(own_key, (), max(1, total - bound), min(bound, total - 1) + 1)
        return jnp.stack([one, total - one])
    lengths = jnp.asarray(length_profile(number_of, total, bound, lean), jnp.int32)
    pairs = (number_of - 1) // 2
    donor, sink = lengths[1:1 + 2 * pairs:2], lengths[2:2 + 2 * pairs:2]
    margin = jnp.minimum(donor - 1, bound - sink)
    passed = jax.random.randint(jax.random.fold_in(own_key, 1), (pairs,), 0, 1 << 20) % (margin + 1)
    lengths = lengths.at[1:1 + 2 * pairs:2].set(donor - passed).at[2:2 + 2 * pairs:2].set(sink + passed)
    return lengths[jax.random.permutation(jax.random.fold_in(own_key, 2), number_of)]


def centred(key, dims, spread, bound, shards=(), kind=jnp.bfloat16):
    values = jax.random.normal(key, dims, jnp.float32) * spread
    if len(shards) > 0:
        values = steps_of(key, dims, shards, -0.22, 0.18) * values
    return jnp.clip(values, min=-bound, max=bound).astype(kind)


def setup_inputs(seed: int = 0, part: int = 0) -> dict:
    keys = jax.random.split(jax.random.key(seed), 6)
    part_splits = jax.random.split(jax.random.fold_in(keys[5], part), 6)
    activations = centred(part_splits[0], (TOKENS, D), 1.0, 6.0, ((0, 4), (1, 4)))
    out_grads = centred(part_splits[1], (TOKENS, F), 1.0, 6.0, ((0, 4), (1, 4)))
    eigvecs = centred(keys[2], (EIGS, D, F), (D * F) ** -0.5, 0.0007324219, ((0, 4), (1, 4)), jnp.float32)
    eigvals = jnp.clip(jnp.exp(jax.random.uniform(keys[3], (EIGS,), jnp.float32, math.log(0.5), math.log(4.0))), 0.5, 4.0)
    segment_ids = jnp.searchsorted(jnp.cumsum(ragged_sizes(part_splits[4], TOK_DEV * N_BLK // SEG_MEAN, TOKENS, SEG_MOST, 2)), jnp.arange(TOKENS), side="right").astype(jnp.int32)
    return {"activations": activations, "out_grads": out_grads, "eigvecs": eigvecs, "eigvals": eigvals, "segment_ids": segment_ids}


def reference(activations, out_grads, eigvecs, eigvals, segment_ids):
    widened = activations.astype(jnp.float32)

    def one_slab(slab):
        rounded = slab.astype(jnp.bfloat16)
        projected = lax.dot_general(out_grads, rounded, (((1,), (1,)), ((), ())), preferred_element_type=jnp.float32)
        return jnp.sum(projected * widened, axis=1)

    token_scores = lax.map(one_slab, eigvecs)
    member = (segment_ids[:, None] == jnp.arange(EXAMPLES, dtype=jnp.int32)[None, :]).astype(jnp.float32)
    scores = jnp.dot(member.T, token_scores.T, precision=lax.Precision.HIGHEST)
    return scores / eigvals[None, :]
```

```python
import jax
import jax.numpy as jnp
from jax import lax
from jax.experimental import pallas as pl
from jax.experimental.pallas import tpu as pltpu
from jax.sharding import PartitionSpec as P

SEG_MEAN = 16
QUARTERS = 4
PLANES = 4
INNER, OUTER, ACROSS, SIBLING = 0, 1, 2, 3


def passed_along(array, axis, by):
    length = lax.axis_size(axis)
    return lax.ppermute(array, axis, [(i, (i + by) % length) for i in range(length)])


def by_ring(activations, out_grads, eigvecs, eigvals, segment_ids):
    tok_rows = activations.shape[0]
    blocks = lax.axis_size("blk")
    mine = lax.axis_index("blk")
    number = eigvals.shape[0]
    examples = tok_rows * blocks // SEG_MEAN
    widened = activations.astype(jnp.float32)
    slab = eigvecs[0].astype(jnp.bfloat16)
    grads = lax.all_gather(out_grads, "rows", axis=1, tiled=True)
    columns = jnp.arange(number, dtype=jnp.int32)

    def score(piece, owner, totals):
        projected = lax.dot_general(
            grads, piece, (((1,), (1,)), ((), ())), preferred_element_type=jnp.float32
        )
        partial_sum = jnp.sum(projected * widened, axis=1)
        picked = (columns == owner).astype(jnp.float32)
        return totals + partial_sum[:, None] * picked[None, :]

    totals = score(slab, mine, jnp.zeros((tok_rows, number), jnp.float32))
    moving = slab
    for step in range(blocks - 1):
        moving = passed_along(moving, "blk", 1)
        totals = score(moving, (mine - step - 1) % blocks, totals)
    member = (segment_ids[:, None] == jnp.arange(examples, dtype=jnp.int32)[None, :]).astype(
        jnp.float32
    )
    full_tokens = lax.psum(totals, "rows")
    local_scores = jnp.dot(member.T, full_tokens, precision=lax.Precision.HIGHEST)
    scores = lax.psum(local_scores, "blk")
    return scores / eigvals[None, :]


def kernel(
    a_ref, g_ref, e_ref, out_ref, all_g,
    slab, acts, held, stage,
    got_g, sent_g, got_a, sent_a, local_sem, stage_sem,
):
    blk = lax.axis_index("blk")
    z = lax.axis_index("rows")
    half, core = blk // 2, blk % 2
    upper = z >= PLANES // 2
    toward = jnp.where(upper, -1, 1)
    is_end = (z == 0) | (z == PLANES - 1)
    is_mid = jnp.logical_not(is_end)
    here = jnp.where(is_end, 0, 1)

    def plane(m):
        return jnp.where(upper, PLANES - 1 - m, m)

    across = {"blk": (1 - half) * 2 + core}
    sibling = {"blk": half * 2 + 1 - core}
    inner = {"rows": z + toward}
    outer = {"rows": jnp.where(is_mid, z - toward, z + toward)}
    targets = {INNER: inner, OUTER: outer, ACROSS: across, SIBLING: sibling}

    toks = a_ref.shape[0]
    quarter = toks // QUARTERS
    width = g_ref.shape[1]
    depth = slab.shape[1]

    def unit(h, c, m, q):
        rows = pl.ds(pl.multiple_of(c * toks + q * quarter, 16), quarter)
        return all_g.at[h, plane(m), rows]

    def sending(channel, other, m, q, own=False):
        h = jnp.where(other == 1, 1 - half, half)
        dst = unit(h, core, m, q)
        src = g_ref.at[pl.ds(pl.multiple_of(q * quarter, 16), quarter)] if own else dst
        return pltpu.make_async_remote_copy(
            src_ref=src,
            dst_ref=dst,
            send_sem=sent_g.at[channel, other, plane(m), q],
            recv_sem=got_g.at[h, core, plane(m), q],
            device_id=targets[channel],
            device_id_type=pl.DeviceIdType.MESH,
        )

    def await_unit(other, c, m, q):
        h = jnp.where(other == 1, 1 - half, half)
        piece = unit(h, c, m, q)
        pltpu.make_async_copy(piece, piece, got_g.at[h, c, plane(m), q]).wait()

    def act_rows(h, c):
        return acts.at[h, pl.ds(pl.multiple_of(c * toks, 16), toks)]

    def act_send(index, target, h, src):
        return pltpu.make_async_remote_copy(
            src_ref=src,
            dst_ref=act_rows(h, core),
            send_sem=sent_a.at[index],
            recv_sem=got_a.at[h, core],
            device_id=target,
            device_id_type=pl.DeviceIdType.MESH,
        )

    def await_acts(h, c):
        rows = act_rows(h, c)
        pltpu.make_async_copy(rows, rows, got_a.at[h, c]).wait()

    barrier = pltpu.get_barrier_semaphore()
    for target in (inner, across, sibling):
        pl.semaphore_signal(barrier, inc=1, device_id=target, device_id_type=pl.DeviceIdType.MESH)

    @pl.when(is_mid)
    def _():
        pl.semaphore_signal(barrier, inc=1, device_id=outer, device_id_type=pl.DeviceIdType.MESH)

    pl.semaphore_wait(barrier, jnp.where(is_mid, 4, 3))

    act_send(0, across, half, a_ref).start()
    act_send(1, sibling, half, a_ref).start()

    @pl.loop(0, QUARTERS)
    def _(q):
        sending(INNER, 0, here, q, own=True).start()

        @pl.when(is_mid)
        def _():
            sending(OUTER, 0, here, q, own=True).start()

        sending(ACROSS, 0, here, q, own=True).start()
        sending(SIBLING, 0, here, q, own=True).start()

    own_acts = pltpu.make_async_copy(a_ref, act_rows(half, core), local_sem.at[0])
    own_acts.start()
    own_grads = pltpu.make_async_copy(
        g_ref,
        all_g.at[half, z, pl.ds(pl.multiple_of(core * toks, 16), toks)],
        local_sem.at[1],
    )
    own_grads.start()

    chunk = stage.shape[1]
    per_piece = depth // chunk
    chunks = per_piece * PLANES

    def fetch(i):
        rows = pl.ds(pl.multiple_of((i % per_piece) * chunk, chunk), chunk)
        cols = pl.ds(pl.multiple_of((i // per_piece) * width, 128), width)
        return pltpu.make_async_copy(e_ref.at[0, rows, cols], stage.at[i % 2], stage_sem.at[i % 2])

    fetch(0).start()

    @pl.loop(0, chunks)
    def _(i):
        @pl.when(i + 1 < chunks)
        def _():
            fetch(i + 1).start()

        fetch(i).wait()
        rows = pl.ds(pl.multiple_of((i % per_piece) * chunk, chunk), chunk)
        slab[i // per_piece, rows, :] = stage[i % 2].astype(jnp.bfloat16)

    out_ref[...] = jnp.zeros_like(out_ref)
    own_acts.wait()
    own_grads.wait()
    await_acts(1 - half, core)
    act_send(2, sibling, 1 - half, act_rows(1 - half, core)).start()
    await_acts(half, 1 - core)
    await_acts(1 - half, 1 - core)

    tile = 256

    def score(other, m):
        h = jnp.where(other == 1, 1 - half, half)
        p = plane(m)
        load = pltpu.make_async_copy(all_g.at[h, p], held, local_sem.at[2])
        load.start()
        load.wait()

        @pl.loop(0, 2 * (depth // tile))
        def _(i):
            c, d = i % 2, i // 2
            rows = pl.ds(pl.multiple_of(c * toks, 16), toks)
            cols = pl.ds(pl.multiple_of(d * tile, tile), tile)
            projected = lax.dot_general(
                held[rows, :], slab[p, cols, :],
                (((1,), (1,)), ((), ())), preferred_element_type=jnp.float32,
            )
            weighed = projected * acts[h, rows, cols].astype(jnp.float32)
            out_ref[h, rows, :] += weighed[:, :128] + weighed[:, 128:]

    @pl.loop(0, 16)
    def _(s):
        full = s // QUARTERS
        q = s % QUARTERS

        @pl.when(is_end)
        def _():
            @pl.when(s < 12)
            def _():
                await_unit(0, core, 1 + full, q)

                @pl.when((s >= 4) | (s == 3))
                def _():
                    sending(ACROSS, 0, 1 + full, q).start()

                sending(SIBLING, 0, 1 + full, q).start()

            @pl.when((s >= 12) & (s < 15))
            def _():
                await_unit(1, core, 1, q)
                sending(SIBLING, 1, 1, q).start()

            @pl.when(s < 13)
            def _():
                late = s - 5
                m = jnp.where(s < 4, 0, jnp.where(s == 4, 1, 2 + jnp.maximum(late, 0) // QUARTERS))
                part = jnp.where(s < 4, q, jnp.where(s == 4, 3, jnp.maximum(late, 0) % QUARTERS))
                await_unit(1, core, m, part)

                @pl.when(s < 4)
                def _():
                    sending(INNER, 1, 0, q).start()

                sending(SIBLING, 1, m, part).start()

        @pl.when(is_mid)
        def _():
            @pl.when(s < 8)
            def _():
                await_unit(0, core, 2 + full, q)
                sending(OUTER, 0, 2 + full, q).start()
                sending(ACROSS, 0, 2 + full, q).start()
                sending(SIBLING, 0, 2 + full, q).start()

            @pl.when(s < 4)
            def _():
                await_unit(0, core, 0, q)
                sending(INNER, 0, 0, q).start()
                sending(SIBLING, 0, 0, q).start()

            @pl.when((s >= 4) & (s < 8))
            def _():
                await_unit(1, core, 0, q)
                sending(SIBLING, 1, 0, q).start()

            @pl.when(s < 12)
            def _():
                await_unit(1, core, 1 + full, q)
                sending(SIBLING, 1, 1 + full, q).start()

            @pl.when((s >= 8) & (s < 11))
            def _():
                sending(OUTER, 1, 1, q).start()

        end_turn = [(1, 0, 0), (4, 0, 1), (5, 1, 0), (8, 0, 2), (9, 1, 2), (12, 0, 3), (13, 1, 3), (15, 1, 1)]
        mid_turn = [(1, 0, 1), (4, 0, 0), (5, 0, 2), (8, 1, 1), (9, 0, 3), (12, 1, 0), (13, 1, 2), (15, 1, 3)]
        other, m, due = jnp.int32(0), jnp.int32(0), s < 0
        for (at, end_other, end_m), (_, mid_other, mid_m) in zip(end_turn, mid_turn):
            other = jnp.where(s == at, jnp.where(is_end, end_other, mid_other), other)
            m = jnp.where(s == at, jnp.where(is_end, end_m, mid_m), m)
            due = due | (s == at)

        @pl.when(due)
        def _():
            @pl.loop(0, QUARTERS)
            def _(part):
                await_unit(other, 1 - core, m, part)

            score(other, m)

    for index in range(3):
        act_send(index, sibling, half, a_ref).wait_send()

    @pl.loop(0, PLANES * QUARTERS)
    def _(i):
        m, q = i // QUARTERS, i % QUARTERS
        sending(SIBLING, 0, m, q).wait_send()
        sending(SIBLING, 1, m, q).wait_send()

        @pl.when(is_end)
        def _():
            @pl.when(m == 0)
            def _():
                sending(INNER, 0, m, q).wait_send()
                sending(INNER, 1, m, q).wait_send()

            @pl.when((m != 1) | (q == 3))
            def _():
                sending(ACROSS, 0, m, q).wait_send()

        @pl.when(is_mid)
        def _():
            @pl.when(m < 2)
            def _():
                sending(INNER, 0, m, q).wait_send()

            @pl.when(m > 0)
            def _():
                sending(OUTER, 0, m, q).wait_send()
                sending(ACROSS, 0, m, q).wait_send()

            @pl.when((m == 1) & (q < 3))
            def _():
                sending(OUTER, 1, m, q).wait_send()


def by_kernel(activations, out_grads, eigvecs, eigvals, segment_ids):
    toks, depth = activations.shape
    width = out_grads.shape[1]
    blocks = lax.axis_size("blk")
    number = eigvals.shape[0]
    examples = toks * blocks // SEG_MEAN
    any_space = pl.BlockSpec(memory_space=pl.ANY)
    token_sums, _ = pl.pallas_call(
        kernel,
        out_shape=(
            jax.ShapeDtypeStruct((2, 2 * toks, 128), jnp.float32),
            jax.ShapeDtypeStruct((2, PLANES, 2 * toks, width), jnp.bfloat16),
        ),
        in_specs=[any_space] * 3,
        out_specs=(pl.BlockSpec(memory_space=pltpu.VMEM), any_space),
        scratch_shapes=[
            pltpu.VMEM((PLANES, depth, width), jnp.bfloat16),
            pltpu.VMEM((2, 2 * toks, depth), jnp.bfloat16),
            pltpu.VMEM((2 * toks, width), jnp.bfloat16),
            pltpu.VMEM((2, min(128, depth), width), jnp.float32),
            pltpu.SemaphoreType.DMA((2, 2, PLANES, QUARTERS)),
            pltpu.SemaphoreType.DMA((4, 2, PLANES, QUARTERS)),
            pltpu.SemaphoreType.DMA((2, 2)),
            pltpu.SemaphoreType.DMA((3,)),
            pltpu.SemaphoreType.DMA((3,)),
            pltpu.SemaphoreType.DMA((2,)),
        ],
        compiler_params=pltpu.CompilerParams(
            collective_id=0, has_side_effects=True, vmem_limit_bytes=60 * 2**20
        ),
        cost_estimate=pl.CostEstimate(
            flops=2 * blocks * toks * depth * width * PLANES,
            bytes_accessed=4 * depth * width * PLANES + 4 * blocks * toks * width * PLANES,
            transcendentals=0,
        ),
    )(activations, out_grads, eigvecs)
    token_scores = jnp.sum(token_sums.reshape(blocks * toks, 128), axis=1)
    ids = lax.all_gather(segment_ids, "blk", tiled=True)
    member = (ids[:, None] == jnp.arange(examples, dtype=jnp.int32)[None, :]).astype(jnp.float32)
    scored = jnp.dot(member.T, token_scores[:, None], precision=lax.Precision.HIGHEST)
    picked = (jnp.arange(number, dtype=jnp.int32) == lax.axis_index("blk")).astype(jnp.float32)
    scores = lax.psum(scored * picked[None, :], ("blk", "rows"))
    return scores / eigvals[None, :]


def local(activations, out_grads, eigvecs, eigvals, segment_ids):
    toks, depth = activations.shape
    fits = (
        lax.axis_size("blk") == 4
        and lax.axis_size("rows") == PLANES
        and toks % (16 * QUARTERS) == 0
        and out_grads.shape[1] % 128 == 0
        and depth % 256 == 0
    )
    run = by_kernel if fits else by_ring
    return run(activations, out_grads, eigvecs, eigvals, segment_ids)


def solution(mesh):
    in_specs = (
        P(("copies", "blk"), "rows"),
        P(("copies", "blk"), "rows"),
        P("blk", "rows", None),
        P(),
        P(("copies", "blk")),
    )
    out_specs = P("copies", None)
    return jax.shard_map(local, mesh=mesh, in_specs=in_specs, out_specs=out_specs, check_vma=False)
```

```python
import jax
import jax.numpy as jnp
from jax import lax
from jax.experimental import pallas as pl
from jax.experimental.pallas import tpu as pltpu
from jax.sharding import PartitionSpec as P

SEG_MEAN = 16
QUARTERS = 4
PLANES = 4
INNER, OUTER, ACROSS, SIBLING = 0, 1, 2, 3


def passed_along(array, axis, by):
    length = lax.axis_size(axis)
    return lax.ppermute(array, axis, [(i, (i + by) % length) for i in range(length)])


def by_ring(activations, out_grads, eigvecs, eigvals, segment_ids):
    tok_rows = activations.shape[0]
    blocks = lax.axis_size("blk")
    mine = lax.axis_index("blk")
    number = eigvals.shape[0]
    examples = tok_rows * blocks // SEG_MEAN
    widened = activations.astype(jnp.float32)
    slab = eigvecs[0].astype(jnp.bfloat16)
    grads = lax.all_gather(out_grads, "rows", axis=1, tiled=True)
    columns = jnp.arange(number, dtype=jnp.int32)

    def score(piece, owner, totals):
        projected = lax.dot_general(
            grads, piece, (((1,), (1,)), ((), ())), preferred_element_type=jnp.float32
        )
        partial_sum = jnp.sum(projected * widened, axis=1)
        picked = (columns == owner).astype(jnp.float32)
        return totals + partial_sum[:, None] * picked[None, :]

    totals = score(slab, mine, jnp.zeros((tok_rows, number), jnp.float32))
    moving = slab
    for step in range(blocks - 1):
        moving = passed_along(moving, "blk", 1)
        totals = score(moving, (mine - step - 1) % blocks, totals)
    member = (segment_ids[:, None] == jnp.arange(examples, dtype=jnp.int32)[None, :]).astype(
        jnp.float32
    )
    full_tokens = lax.psum(totals, "rows")
    local_scores = jnp.dot(member.T, full_tokens, precision=lax.Precision.HIGHEST)
    scores = lax.psum(local_scores, "blk")
    return scores / eigvals[None, :]


def turns(s_list):
    return {2 * s + i: job for s, jobs in s_list.items() for i, job in enumerate(jobs)}


END_TURNS = turns({
    0: [(0, 0, 0, 0), (0, 0, 1, 0)],
    2: [(0, 1, 0, 0)],
    3: [(1, 0, 0, 0)],
    4: [(0, 1, 1, 0), (1, 0, 1, 0)],
    6: [(0, 2, 0, 0)],
    7: [(1, 2, 0, 0)],
    8: [(0, 2, 1, 0)],
    9: [(1, 2, 1, 0), (1, 1, 0, 0)],
    10: [(1, 1, 1, 0)],
})
MID_TURNS = turns({
    0: [(0, 1, 0, 0), (0, 1, 1, 0)],
    2: [(0, 0, 0, 0)],
    3: [(0, 2, 0, 0)],
    4: [(0, 0, 1, 0), (0, 2, 1, 0)],
    5: [(1, 1, 0, 0)],
    6: [(1, 1, 1, 0), (0, 3, 0, 0)],
    7: [(1, 0, 0, 0)],
    8: [(0, 3, 1, 0)],
    9: [(1, 3, 0, 0)],
    10: [(1, 2, 0, 0), (1, 3, 1, 0)],
    11: [(0, 3, 0, 1), (0, 3, 1, 1)],
    12: [(1, 3, 0, 1), (1, 3, 1, 1)],
    13: [(1, 2, 1, 0), (1, 0, 1, 0)],
})
STEPS = 14


def kernel(
    a_ref, g_ref, e_ref, i_ref, out_ref, all_g,
    slab, acts, held, stage, sums, ids, by_plane, by_block,
    got_g, sent_g, got_a, sent_a, got_v, sent_v, got_i, sent_i, got_s, sent_s, local_sem, stage_sem,
):
    mesh_id = pl.DeviceIdType.MESH
    blk = lax.axis_index("blk")
    z = lax.axis_index("rows")
    y = lax.axis_index("copies")
    half, core = blk // 2, blk % 2
    upper = z >= PLANES // 2
    toward = jnp.where(upper, -1, 1)
    is_end = (z == 0) | (z == PLANES - 1)
    is_mid = jnp.logical_not(is_end)
    here = jnp.where(is_end, 0, 1)

    def plane(m):
        return jnp.where(upper, PLANES - 1 - m, m)

    across = {"blk": (1 - half) * 2 + core}
    sibling = {"blk": half * 2 + 1 - core}
    inner = {"rows": z + toward}
    outer = {"rows": jnp.where(is_mid, z - toward, z + toward)}
    beside = {"copies": 1 - y}
    targets = {INNER: inner, OUTER: outer, ACROSS: across, SIBLING: sibling}

    toks = a_ref.shape[0]
    quarter = toks // QUARTERS
    width = g_ref.shape[1]
    depth = slab.shape[1]

    def unit(h, c, m, q):
        rows = pl.ds(pl.multiple_of(c * toks + q * quarter, 16), quarter)
        return all_g.at[h, plane(m), rows]

    def column(other):
        return jnp.where(other == 1, 1 - half, half)

    def sending(channel, other, m, q, own=False):
        h = column(other)
        dst = unit(h, core, m, q)
        src = g_ref.at[pl.ds(pl.multiple_of(q * quarter, 16), quarter)] if own else dst
        return pltpu.make_async_remote_copy(
            src_ref=src,
            dst_ref=dst,
            send_sem=sent_g.at[channel, other, plane(m), q],
            recv_sem=got_g.at[h, core, plane(m), q],
            device_id=targets[channel],
            device_id_type=mesh_id,
        )

    def await_unit(other, c, m, q):
        h = column(other)
        piece = unit(h, c, m, q)
        pltpu.make_async_copy(piece, piece, got_g.at[h, c, plane(m), q]).wait()

    def act_rows(h, c):
        return acts.at[h, pl.ds(pl.multiple_of(c * toks, 16), toks)]

    def act_send(index, target, h, src):
        return pltpu.make_async_remote_copy(
            src_ref=src,
            dst_ref=act_rows(h, core),
            send_sem=sent_a.at[index],
            recv_sem=got_a.at[h, core],
            device_id=target,
            device_id_type=mesh_id,
        )

    def await_acts(h, c):
        rows = act_rows(h, c)
        pltpu.make_async_copy(rows, rows, got_a.at[h, c]).wait()

    strip = depth // 2 // QUARTERS

    def strip_rows(which, u):
        return pl.ds(pl.multiple_of(which * (depth // 2) + u * strip, 16), strip)

    def slab_send(target, source, u):
        return pltpu.make_async_remote_copy(
            src_ref=slab.at[source, strip_rows(y, u)],
            dst_ref=slab.at[PLANES, strip_rows(y, u)],
            send_sem=sent_v.at[u],
            recv_sem=got_v.at[y, u],
            device_id=target,
            device_id_type=mesh_id,
        )

    def await_slab(which, u):
        rows = slab.at[PLANES, strip_rows(which, u)]
        pltpu.make_async_copy(rows, rows, got_v.at[which, u]).wait()

    def ids_send(j):
        return pltpu.make_async_remote_copy(
            src_ref=i_ref,
            dst_ref=ids.at[blk],
            send_sem=sent_i.at[j - 1],
            recv_sem=got_i.at[blk],
            device_id={"blk": (blk + j) % 4},
            device_id_type=mesh_id,
        )

    barrier = pltpu.get_barrier_semaphore()
    for j in range(1, 4):
        for target in ({"blk": (blk + j) % 4}, {"rows": (z + j) % PLANES}):
            pl.semaphore_signal(barrier, inc=1, device_id=target, device_id_type=mesh_id)
    pl.semaphore_signal(barrier, inc=1, device_id=beside, device_id_type=mesh_id)
    pl.semaphore_wait(barrier, 7)

    act_send(0, across, half, a_ref).start()
    act_send(1, sibling, half, a_ref).start()

    @pl.loop(0, QUARTERS)
    def _(q):
        sending(INNER, 0, here, q, own=True).start()

        @pl.when(is_mid)
        def _():
            sending(OUTER, 0, here, q, own=True).start()

        sending(ACROSS, 0, here, q, own=True).start()
        sending(SIBLING, 0, here, q, own=True).start()

    for j in range(1, 4):
        ids_send(j).start()

    @pl.when(is_end)
    def _():
        act_send(3, inner, 2 + half, a_ref).start()

    own_acts = pltpu.make_async_copy(a_ref, act_rows(half, core), local_sem.at[0])
    own_acts.start()
    own_grads = pltpu.make_async_copy(
        g_ref,
        all_g.at[half, z, pl.ds(pl.multiple_of(core * toks, 16), toks)],
        local_sem.at[1],
    )
    own_grads.start()

    chunk = stage.shape[1]
    per_piece = depth // chunk
    chunks = per_piece * PLANES

    def fetch_piece(i):
        return plane((PLANES - 1 + i // per_piece) % PLANES)

    def fetch(i):
        rows = pl.ds(pl.multiple_of((i % per_piece) * chunk, chunk), chunk)
        cols = pl.ds(pl.multiple_of(fetch_piece(i) * width, 128), width)
        return pltpu.make_async_copy(e_ref.at[0, rows, cols], stage.at[i % 2], stage_sem.at[i % 2])

    fetch(0).start()

    @pl.loop(0, chunks)
    def _(i):
        @pl.when(i + 1 < chunks)
        def _():
            fetch(i + 1).start()

        fetch(i).wait()
        rows = pl.ds(pl.multiple_of((i % per_piece) * chunk, chunk), chunk)
        slab[fetch_piece(i), rows, :] = stage[i % 2].astype(jnp.bfloat16)

        @pl.when((i == per_piece - 1) & is_end)
        def _():
            @pl.loop(0, QUARTERS)
            def _(u):
                slab_send(inner, plane(PLANES - 1), u).start()

    sums[...] = jnp.zeros_like(sums)
    ids[blk] = i_ref[...]
    own_acts.wait()
    own_grads.wait()
    await_acts(1 - half, core)
    act_send(2, sibling, 1 - half, act_rows(1 - half, core)).start()

    @pl.when(is_end)
    def _():
        act_send(4, inner, 2 + 1 - half, act_rows(1 - half, core)).start()

    await_acts(half, 1 - core)
    await_acts(1 - half, 1 - core)

    tile = 256
    part = toks // 2

    def score(other, m, second, for_end):
        h = column(other)
        p = plane(m)
        for c in range(2):
            pltpu.make_async_copy(
                all_g.at[h, p, pl.ds(pl.multiple_of(c * toks + second * part, 16), part)],
                held.at[pl.ds(c * part, part)],
                local_sem.at[2 + c],
            ).start()
        for c in range(2):
            pltpu.make_async_copy(
                all_g.at[h, p, pl.ds(pl.multiple_of(c * toks + second * part, 16), part)],
                held.at[pl.ds(c * part, part)],
                local_sem.at[2 + c],
            ).wait()
        which = jnp.where(for_end == 1, PLANES, p)

        @pl.loop(0, depth // tile)
        def _(d):
            cols = pl.ds(pl.multiple_of(d * tile, tile), tile)
            projected = lax.dot_general(
                held[...], slab[which, cols, :],
                (((1,), (1,)), ((), ())), preferred_element_type=jnp.float32,
            )
            for c in range(2):
                rows = pl.ds(pl.multiple_of(c * toks + second * part, 16), part)
                factor = acts[h + 2 * for_end, rows, cols].astype(jnp.float32)
                weighed = projected[c * part:(c + 1) * part] * factor
                sums[h, rows, :] += weighed[:, :128] + weighed[:, 128:]

    @pl.loop(0, STEPS)
    def _(s):
        full = s // QUARTERS
        q = s % QUARTERS

        @pl.when(is_end)
        def _():
            @pl.when(s < 8)
            def _():
                await_unit(0, core, 1 + full, q)

                @pl.when(s >= 3)
                def _():
                    sending(ACROSS, 0, 1 + full, q).start()

                sending(SIBLING, 0, 1 + full, q).start()

            @pl.when((s >= 8) & (s < 11))
            def _():
                await_unit(1, core, 1, q)
                sending(SIBLING, 1, 1, q).start()

            @pl.when(s < 9)
            def _():
                late = jnp.maximum(s - 5, 0)
                m = jnp.where(s < 4, 0, jnp.where(s == 4, 1, 2))
                r = jnp.where(s < 4, q, jnp.where(s == 4, 3, late))
                await_unit(1, core, m, r)

                @pl.when(s == 3)
                def _():
                    sending(INNER, 1, 0, 3).start()

                sending(SIBLING, 1, m, r).start()

        @pl.when(is_mid)
        def _():
            @pl.when(s < 8)
            def _():
                await_unit(0, core, 2 + full, q)

                @pl.when(s < 4)
                def _():
                    sending(OUTER, 0, 2, q).start()

                @pl.when(s >= 4)
                def _():
                    sending(ACROSS, 0, 3, q).start()

                sending(SIBLING, 0, 2 + full, q).start()

            @pl.when((s >= 8) & (s < 12))
            def _():
                await_unit(1, core, 2, q)
                sending(SIBLING, 1, 2, q).start()

            @pl.when(s < 4)
            def _():
                await_unit(0, core, 0, q)
                sending(INNER, 0, 0, q).start()

                @pl.when(s < 3)
                def _():
                    sending(ACROSS, 0, 0, q).start()

                sending(SIBLING, 0, 0, q).start()

            @pl.when(s < 11)
            def _():
                m = jnp.where(s < 4, 1, jnp.where(s < 7, 0, 3))
                r = jnp.where(s < 7, q, jnp.maximum(s - 7, 0))
                await_unit(1, core, m, r)
                sending(SIBLING, 1, m, r).start()

            @pl.when((s >= 4) & (s < 8))
            def _():
                sending(INNER, 1, 1, q).start()

                @pl.when(s < 7)
                def _():
                    sending(OUTER, 1, 1, q).start()

            @pl.when((s >= 7) & (s < 11))
            def _():
                await_slab(y, s - 7)
                slab_send(beside, PLANES, s - 7).start()

            @pl.when(s == 11)
            def _():
                await_acts(2 + half, core)
                act_send(3, sibling, 2 + half, act_rows(2 + half, core)).start()
                await_acts(2 + 1 - half, core)
                act_send(4, sibling, 2 + 1 - half, act_rows(2 + 1 - half, core)).start()

                @pl.loop(0, QUARTERS)
                def _(u):
                    await_slab(1 - y, u)

                await_acts(2 + half, 1 - core)
                await_acts(2 + 1 - half, 1 - core)

            @pl.when(s == 12)
            def _():
                await_unit(1, core, 0, 3)
                sending(SIBLING, 1, 0, 3).start()

        @pl.loop(0, 2)
        def _(i):
            turn = 2 * s + i
            job = [jnp.int32(0)] * 4
            due = turn < 0
            for at in sorted(set(END_TURNS) | set(MID_TURNS)):
                for table, mine in ((END_TURNS, is_end), (MID_TURNS, is_mid)):
                    if at in table:
                        now = (turn == at) & mine
                        job = [jnp.where(now, new, old) for new, old in zip(table[at], job)]
                        due = due | now
            other, m, second, for_end = job

            @pl.when(due)
            def _():
                @pl.when(for_end == 0)
                def _():
                    await_unit(other, 1 - core, m, 2 * second)
                    await_unit(other, 1 - core, m, 2 * second + 1)

                score(other, m, second, for_end)

    for j in range(1, 4):
        taken = (blk + j) % 4
        pltpu.make_async_copy(ids.at[taken], ids.at[taken], got_i.at[taken]).wait()
    spots = out_ref.shape[1]
    example = lax.broadcasted_iota(jnp.int32, (spots, toks), 0)
    total = jnp.zeros((spots, 128), jnp.float32)
    for b in range(4):
        member = (ids[b, 0:1, :] == example).astype(jnp.float32)
        total += jnp.dot(
            member, sums[b // 2, (b % 2) * toks:(b % 2 + 1) * toks, :],
            precision=lax.Precision.HIGHEST, preferred_element_type=jnp.float32,
        )
    across_lanes = lax.dot_general(
        jnp.ones((8, 128), jnp.float32), total, (((1,), (1,)), ((), ())),
        precision=lax.Precision.HIGHEST, preferred_element_type=jnp.float32,
    )
    mine = lax.broadcasted_iota(jnp.int32, (8, spots), 0) == blk
    by_plane[z] = jnp.where(mine, across_lanes, 0.0)

    def shared(buffer, axis, me, phase):
        def sent(j):
            return pltpu.make_async_remote_copy(
                src_ref=buffer.at[me],
                dst_ref=buffer.at[me],
                send_sem=sent_s.at[phase, j - 1],
                recv_sem=got_s.at[phase, me],
                device_id={axis: (me + j) % 4},
                device_id_type=mesh_id,
            )

        for j in range(1, 4):
            sent(j).start()
        for j in range(1, 4):
            slot = (me + j) % 4
            pltpu.make_async_copy(buffer.at[slot], buffer.at[slot], got_s.at[phase, slot]).wait()
        result = (buffer[0] + buffer[1]) + (buffer[2] + buffer[3])
        for j in range(1, 4):
            sent(j).wait_send()
        return result

    by_block[blk] = shared(by_plane, "rows", z, 0)
    out_ref[...] = shared(by_block, "blk", blk, 1)

    for j in range(1, 4):
        ids_send(j).wait_send()
    for index in range(5):
        act_send(index, sibling, half, a_ref).wait_send()

    @pl.loop(0, QUARTERS)
    def _(u):
        slab_send(beside, PLANES, u).wait_send()

    @pl.loop(0, PLANES * QUARTERS)
    def _(i):
        m, q = i // QUARTERS, i % QUARTERS

        @pl.when(is_mid | (m < 3))
        def _():
            sending(SIBLING, 0, m, q).wait_send()
            sending(SIBLING, 1, m, q).wait_send()

        @pl.when(is_end)
        def _():
            @pl.when(m == 0)
            def _():
                sending(INNER, 0, m, q).wait_send()

                @pl.when(q == 3)
                def _():
                    sending(INNER, 1, m, q).wait_send()

            @pl.when((m == 0) | (m == 2) | ((m == 1) & (q == 3)))
            def _():
                sending(ACROSS, 0, m, q).wait_send()

        @pl.when(is_mid)
        def _():
            @pl.when(m < 2)
            def _():
                sending(INNER, 0, m, q).wait_send()

            @pl.when((m == 1) | (m == 2))
            def _():
                sending(OUTER, 0, m, q).wait_send()

            @pl.when(m == 1)
            def _():
                sending(INNER, 1, m, q).wait_send()

                @pl.when(q < 3)
                def _():
                    sending(OUTER, 1, m, q).wait_send()

            @pl.when((m == 1) | (m == 3) | ((m == 0) & (q < 3)))
            def _():
                sending(ACROSS, 0, m, q).wait_send()


def by_kernel(activations, out_grads, eigvecs, eigvals, segment_ids):
    toks, depth = activations.shape
    width = out_grads.shape[1]
    blocks = lax.axis_size("blk")
    number = eigvals.shape[0]
    examples = toks * blocks // SEG_MEAN
    spots = -(-examples // 128) * 128
    any_space = pl.BlockSpec(memory_space=pl.ANY)
    in_vmem = pl.BlockSpec(memory_space=pltpu.VMEM)
    scores, _ = pl.pallas_call(
        kernel,
        out_shape=(
            jax.ShapeDtypeStruct((8, spots), jnp.float32),
            jax.ShapeDtypeStruct((2, PLANES, 2 * toks, width), jnp.bfloat16),
        ),
        in_specs=[any_space] * 3 + [in_vmem],
        out_specs=(in_vmem, any_space),
        scratch_shapes=[
            pltpu.VMEM((PLANES + 1, depth, width), jnp.bfloat16),
            pltpu.VMEM((4, 2 * toks, depth), jnp.bfloat16),
            pltpu.VMEM((toks, width), jnp.bfloat16),
            pltpu.VMEM((2, 64, width), jnp.float32),
            pltpu.VMEM((2, 2 * toks, 128), jnp.float32),
            pltpu.VMEM((4, 8, toks), jnp.int32),
            pltpu.VMEM((4, 8, spots), jnp.float32),
            pltpu.VMEM((4, 8, spots), jnp.float32),
            pltpu.SemaphoreType.DMA((2, 2, PLANES, QUARTERS)),
            pltpu.SemaphoreType.DMA((4, 2, PLANES, QUARTERS)),
            pltpu.SemaphoreType.DMA((4, 2)),
            pltpu.SemaphoreType.DMA((5,)),
            pltpu.SemaphoreType.DMA((2, QUARTERS)),
            pltpu.SemaphoreType.DMA((QUARTERS,)),
            pltpu.SemaphoreType.DMA((4,)),
            pltpu.SemaphoreType.DMA((3,)),
            pltpu.SemaphoreType.DMA((2, 4)),
            pltpu.SemaphoreType.DMA((2, 3)),
            pltpu.SemaphoreType.DMA((4,)),
            pltpu.SemaphoreType.DMA((2,)),
        ],
        compiler_params=pltpu.CompilerParams(
            collective_id=0, has_side_effects=True, vmem_limit_bytes=60 * 2**20
        ),
        cost_estimate=pl.CostEstimate(
            flops=2 * blocks * toks * depth * width * PLANES,
            bytes_accessed=4 * depth * width * PLANES + 4 * blocks * toks * width * PLANES,
            transcendentals=0,
        ),
    )(activations, out_grads, eigvecs, jnp.broadcast_to(segment_ids[None, :], (8, toks)))
    return scores[:number, :examples].T / eigvals[None, :]


def local(activations, out_grads, eigvecs, eigvals, segment_ids):
    toks, depth = activations.shape
    fits = (
        lax.axis_size("blk") == 4
        and lax.axis_size("copies") == 2
        and eigvals.shape[0] == 4
        and lax.axis_size("rows") == PLANES
        and toks % (16 * QUARTERS) == 0
        and out_grads.shape[1] % 128 == 0
        and depth % 256 == 0
    )
    run = by_kernel if fits else by_ring
    return run(activations, out_grads, eigvecs, eigvals, segment_ids)


def solution(mesh):
    in_specs = (
        P(("copies", "blk"), "rows"),
        P(("copies", "blk"), "rows"),
        P("blk", "rows", None),
        P(),
        P(("copies", "blk")),
    )
    out_specs = P("copies", None)
    return jax.shard_map(local, mesh=mesh, in_specs=in_specs, out_specs=out_specs, check_vma=False)
```

```python
import jax
import jax.numpy as jnp
from jax import lax
from jax.experimental import pallas as pl
from jax.experimental.pallas import tpu as pltpu
from jax.sharding import PartitionSpec as P

SEG_MEAN = 16
QUARTERS = 4
PLANES = 4
INNER, OUTER, ACROSS, SIBLING = 0, 1, 2, 3


def passed_along(array, axis, by):
    length = lax.axis_size(axis)
    return lax.ppermute(array, axis, [(i, (i + by) % length) for i in range(length)])


def by_ring(activations, out_grads, eigvecs, eigvals, segment_ids):
    tok_rows = activations.shape[0]
    blocks = lax.axis_size("blk")
    mine = lax.axis_index("blk")
    number = eigvals.shape[0]
    examples = tok_rows * blocks // SEG_MEAN
    widened = activations.astype(jnp.float32)
    slab = eigvecs[0].astype(jnp.bfloat16)
    grads = lax.all_gather(out_grads, "rows", axis=1, tiled=True)
    columns = jnp.arange(number, dtype=jnp.int32)

    def score(piece, owner, totals):
        projected = lax.dot_general(
            grads, piece, (((1,), (1,)), ((), ())), preferred_element_type=jnp.float32
        )
        partial_sum = jnp.sum(projected * widened, axis=1)
        picked = (columns == owner).astype(jnp.float32)
        return totals + partial_sum[:, None] * picked[None, :]

    totals = score(slab, mine, jnp.zeros((tok_rows, number), jnp.float32))
    moving = slab
    for step in range(blocks - 1):
        moving = passed_along(moving, "blk", 1)
        totals = score(moving, (mine - step - 1) % blocks, totals)
    member = (segment_ids[:, None] == jnp.arange(examples, dtype=jnp.int32)[None, :]).astype(
        jnp.float32
    )
    full_tokens = lax.psum(totals, "rows")
    local_scores = jnp.dot(member.T, full_tokens, precision=lax.Precision.HIGHEST)
    scores = lax.psum(local_scores, "blk")
    return scores / eigvals[None, :]


AT_ONCE = 4


def turns(s_list):
    return {AT_ONCE * s + i: job for s, jobs in s_list.items() for i, job in enumerate(jobs)}


END_TURNS = turns({
    0: [(0, 0, 0, 0), (0, 0, 1, 0)],
    2: [(0, 1, 0, 0)],
    3: [(1, 0, 0, 0)],
    4: [(0, 1, 1, 0), (1, 0, 1, 0)],
    6: [(0, 2, 0, 0)],
    7: [(1, 2, 0, 0)],
    8: [(0, 2, 1, 0)],
    9: [(1, 2, 1, 0), (1, 1, 0, 0)],
    10: [(1, 1, 1, 0)],
})
MID_TURNS = turns({
    0: [(0, 1, 0, 0), (0, 1, 1, 0)],
    2: [(0, 0, 0, 0)],
    3: [(0, 2, 0, 0)],
    4: [(1, 1, 0, 0), (0, 0, 1, 0)],
    5: [(0, 2, 1, 0)],
    6: [(1, 1, 1, 0)],
    7: [(0, 3, 0, 0), (1, 3, 0, 0)],
    8: [(0, 3, 1, 0)],
    9: [(1, 3, 1, 0), (1, 2, 0, 0)],
    10: [(0, 3, 0, 1), (0, 3, 1, 1), (1, 3, 0, 1), (1, 3, 1, 1)],
    11: [(1, 0, 0, 0), (1, 0, 1, 0), (1, 2, 1, 0)],
})
STEPS = 12


def kernel(
    a_ref, g_ref, e_ref, i_ref, out_ref, all_g,
    slab, acts, held, stage, sums, ids, by_plane, by_block,
    got_g, sent_g, got_a, sent_a, got_v, sent_v, got_i, sent_i, got_s, sent_s, local_sem, stage_sem,
):
    mesh_id = pl.DeviceIdType.MESH
    blk = lax.axis_index("blk")
    z = lax.axis_index("rows")
    y = lax.axis_index("copies")
    half, core = blk // 2, blk % 2
    upper = z >= PLANES // 2
    toward = jnp.where(upper, -1, 1)
    is_end = (z == 0) | (z == PLANES - 1)
    is_mid = jnp.logical_not(is_end)
    here = jnp.where(is_end, 0, 1)

    def plane(m):
        return jnp.where(upper, PLANES - 1 - m, m)

    across = {"blk": (1 - half) * 2 + core}
    sibling = {"blk": half * 2 + 1 - core}
    inner = {"rows": z + toward}
    outer = {"rows": jnp.where(is_mid, z - toward, z + toward)}
    beside = {"copies": 1 - y}
    targets = {INNER: inner, OUTER: outer, ACROSS: across, SIBLING: sibling}

    toks = a_ref.shape[0]
    quarter = toks // QUARTERS
    width = g_ref.shape[1]
    depth = slab.shape[1]

    def unit(h, c, m, q):
        rows = pl.ds(pl.multiple_of(c * toks + q * quarter, 16), quarter)
        return all_g.at[h, plane(m), rows]

    def column(other):
        return jnp.where(other == 1, 1 - half, half)

    def sending(channel, other, m, q, own=False):
        h = column(other)
        dst = unit(h, core, m, q)
        src = g_ref.at[pl.ds(pl.multiple_of(q * quarter, 16), quarter)] if own else dst
        return pltpu.make_async_remote_copy(
            src_ref=src,
            dst_ref=dst,
            send_sem=sent_g.at[channel, other, plane(m), q],
            recv_sem=got_g.at[h, core, plane(m), q],
            device_id=targets[channel],
            device_id_type=mesh_id,
        )

    def await_unit(other, c, m, q):
        h = column(other)
        piece = unit(h, c, m, q)
        pltpu.make_async_copy(piece, piece, got_g.at[h, c, plane(m), q]).wait()

    def act_rows(h, c):
        return acts.at[h, pl.ds(pl.multiple_of(c * toks, 16), toks)]

    def act_send(index, target, h, src):
        return pltpu.make_async_remote_copy(
            src_ref=src,
            dst_ref=act_rows(h, core),
            send_sem=sent_a.at[index],
            recv_sem=got_a.at[h, core],
            device_id=target,
            device_id_type=mesh_id,
        )

    def await_acts(h, c):
        rows = act_rows(h, c)
        pltpu.make_async_copy(rows, rows, got_a.at[h, c]).wait()

    strip = depth // 2 // QUARTERS

    def strip_rows(which, u):
        return pl.ds(pl.multiple_of(which * (depth // 2) + u * strip, 16), strip)

    def slab_send(target, source, u):
        return pltpu.make_async_remote_copy(
            src_ref=slab.at[source, strip_rows(y, u)],
            dst_ref=slab.at[PLANES, strip_rows(y, u)],
            send_sem=sent_v.at[u],
            recv_sem=got_v.at[y, u],
            device_id=target,
            device_id_type=mesh_id,
        )

    def await_slab(which, u):
        rows = slab.at[PLANES, strip_rows(which, u)]
        pltpu.make_async_copy(rows, rows, got_v.at[which, u]).wait()

    def ids_send(j):
        return pltpu.make_async_remote_copy(
            src_ref=i_ref,
            dst_ref=ids.at[blk],
            send_sem=sent_i.at[j - 1],
            recv_sem=got_i.at[blk],
            device_id={"blk": (blk + j) % 4},
            device_id_type=mesh_id,
        )

    barrier = pltpu.get_barrier_semaphore()
    for j in range(1, 4):
        for target in ({"blk": (blk + j) % 4}, {"rows": (z + j) % PLANES}):
            pl.semaphore_signal(barrier, inc=1, device_id=target, device_id_type=mesh_id)
    pl.semaphore_signal(barrier, inc=1, device_id=beside, device_id_type=mesh_id)
    pl.semaphore_wait(barrier, 7)

    act_send(0, across, half, a_ref).start()
    act_send(1, sibling, half, a_ref).start()

    @pl.loop(0, QUARTERS)
    def _(q):
        sending(INNER, 0, here, q, own=True).start()

        @pl.when(is_mid)
        def _():
            sending(OUTER, 0, here, q, own=True).start()

        sending(ACROSS, 0, here, q, own=True).start()
        sending(SIBLING, 0, here, q, own=True).start()

    for j in range(1, 4):
        ids_send(j).start()

    @pl.when(is_end)
    def _():
        act_send(3, inner, 2 + half, a_ref).start()

    own_acts = pltpu.make_async_copy(a_ref, act_rows(half, core), local_sem.at[0])
    own_acts.start()
    own_grads = pltpu.make_async_copy(
        g_ref,
        all_g.at[half, z, pl.ds(pl.multiple_of(core * toks, 16), toks)],
        local_sem.at[1],
    )
    own_grads.start()

    chunk = stage.shape[1]
    per_piece = depth // chunk
    chunks = per_piece * PLANES

    def fetch_piece(i):
        return plane((PLANES - 1 + i // per_piece) % PLANES)

    def fetch(i):
        rows = pl.ds(pl.multiple_of((i % per_piece) * chunk, chunk), chunk)
        cols = pl.ds(pl.multiple_of(fetch_piece(i) * width, 128), width)
        return pltpu.make_async_copy(e_ref.at[0, rows, cols], stage.at[i % 2], stage_sem.at[i % 2])

    fetch(0).start()

    @pl.loop(0, chunks)
    def _(i):
        @pl.when(i + 1 < chunks)
        def _():
            fetch(i + 1).start()

        fetch(i).wait()
        rows = pl.ds(pl.multiple_of((i % per_piece) * chunk, chunk), chunk)
        slab[fetch_piece(i), rows, :] = stage[i % 2].astype(jnp.bfloat16)

        @pl.when((i == per_piece - 1) & is_end)
        def _():
            @pl.loop(0, QUARTERS)
            def _(u):
                slab_send(inner, plane(PLANES - 1), u).start()

    sums[...] = jnp.zeros_like(sums)
    ids[blk] = i_ref[...]
    own_acts.wait()
    own_grads.wait()
    await_acts(1 - half, core)
    act_send(2, sibling, 1 - half, act_rows(1 - half, core)).start()

    @pl.when(is_end)
    def _():
        act_send(4, inner, 2 + 1 - half, act_rows(1 - half, core)).start()

    await_acts(half, 1 - core)
    await_acts(1 - half, 1 - core)

    tile = 256
    part = toks // 2

    def loads(job, slot):
        other, m, second, _ = job
        return [
            pltpu.make_async_copy(
                all_g.at[column(other), plane(m), pl.ds(pl.multiple_of(c * toks + second * part, 16), part)],
                held.at[slot, pl.ds(c * part, part)],
                local_sem.at[2 + 2 * slot + c],
            )
            for c in range(2)
        ]

    def begin(job, slot):
        other, m, second, for_end = job

        @pl.when(for_end == 0)
        def _():
            await_unit(other, 1 - core, m, 2 * second)
            await_unit(other, 1 - core, m, 2 * second + 1)

        for load in loads(job, slot):
            load.start()

    def score(job, slot):
        other, m, second, for_end = job
        h = column(other)
        for load in loads(job, slot):
            load.wait()
        which = jnp.where(for_end == 1, PLANES, plane(m))

        @pl.loop(0, depth // tile)
        def _(d):
            cols = pl.ds(pl.multiple_of(d * tile, tile), tile)
            projected = lax.dot_general(
                held[slot], slab[which, cols, :],
                (((1,), (1,)), ((), ())), preferred_element_type=jnp.float32,
            )
            for c in range(2):
                rows = pl.ds(pl.multiple_of(c * toks + second * part, 16), part)
                factor = acts[h + 2 * for_end, rows, cols].astype(jnp.float32)
                weighed = projected[c * part:(c + 1) * part] * factor
                sums[h, rows, :] += weighed[:, :128] + weighed[:, 128:]

    def job_at(turn):
        job = [jnp.int32(0)] * 4
        for at in sorted(set(END_TURNS) | set(MID_TURNS)):
            for table, mine in ((END_TURNS, is_end), (MID_TURNS, is_mid)):
                if at in table:
                    now = (turn == at) & mine
                    job = [jnp.where(now, new, old) for new, old in zip(table[at], job)]
        return job

    def jobs_in(step):
        count = jnp.int32(0)
        for at in range(STEPS):
            counts = [
                sum(at * AT_ONCE + i in table for i in range(AT_ONCE)) for table in (END_TURNS, MID_TURNS)
            ]
            count = jnp.where(step == at, jnp.where(is_end, counts[0], counts[1]), count)
        return count

    @pl.loop(0, STEPS)
    def _(s):
        full = s // QUARTERS
        q = s % QUARTERS

        @pl.when(is_end)
        def _():
            @pl.when(s < 8)
            def _():
                await_unit(0, core, 1 + full, q)

                @pl.when(s >= 3)
                def _():
                    sending(ACROSS, 0, 1 + full, q).start()

                sending(SIBLING, 0, 1 + full, q).start()

            @pl.when((s >= 8) & (s < 11))
            def _():
                await_unit(1, core, 1, q)
                sending(SIBLING, 1, 1, q).start()

            @pl.when(s < 9)
            def _():
                late = jnp.maximum(s - 5, 0)
                m = jnp.where(s < 4, 0, jnp.where(s == 4, 1, 2))
                r = jnp.where(s < 4, q, jnp.where(s == 4, 3, late))
                await_unit(1, core, m, r)

                @pl.when(s == 3)
                def _():
                    sending(INNER, 1, 0, 3).start()

                sending(SIBLING, 1, m, r).start()

        @pl.when(is_mid)
        def _():
            @pl.when(s < 8)
            def _():
                await_unit(0, core, 2 + full, q)

                @pl.when(s < 4)
                def _():
                    sending(OUTER, 0, 2, q).start()

                @pl.when(s >= 4)
                def _():
                    sending(ACROSS, 0, 3, q).start()

                sending(SIBLING, 0, 2 + full, q).start()

            @pl.when((s >= 8) & (s < 12))
            def _():
                await_unit(1, core, 2, q)
                sending(SIBLING, 1, 2, q).start()

            @pl.when(s < 4)
            def _():
                await_unit(0, core, 0, q)
                sending(INNER, 0, 0, q).start()

                @pl.when(s == 0)
                def _():
                    sending(ACROSS, 0, 0, 0).start()

                sending(SIBLING, 0, 0, q).start()

            @pl.when((s >= 1) & (s < 12))
            def _():
                turn = jnp.maximum(s - 1, 0)
                m = jnp.where(turn < 4, 1, jnp.where((turn == 4) | (turn > 8), 0, 3))
                r = jnp.where(turn < 5, turn % QUARTERS, (turn - 5 + 5 * QUARTERS) % QUARTERS)
                r = jnp.where(turn > 8, turn - 8, r)
                await_unit(1, core, m, r)
                sending(SIBLING, 1, m, r).start()

            @pl.when((s >= 8) & (s < 10))
            def _():
                sending(ACROSS, 0, 0, jnp.maximum(s - 7, 0)).start()

            @pl.when((s >= 4) & (s < 8))
            def _():
                sending(INNER, 1, 1, q).start()

                @pl.when(s < 7)
                def _():
                    sending(OUTER, 1, 1, q).start()

            @pl.when((s >= 6) & (s < 10))
            def _():
                u = jnp.maximum(s - 6, 0)
                await_slab(y, u)
                slab_send(beside, PLANES, u).start()

            @pl.when(s == 10)
            def _():
                await_acts(2 + half, core)
                act_send(3, sibling, 2 + half, act_rows(2 + half, core)).start()
                await_acts(2 + 1 - half, core)
                act_send(4, sibling, 2 + 1 - half, act_rows(2 + 1 - half, core)).start()

                @pl.loop(0, QUARTERS)
                def _(u):
                    await_slab(1 - y, u)

                await_acts(2 + half, 1 - core)
                await_acts(2 + 1 - half, 1 - core)

            @pl.when(s == 11)
            def _():
                await_unit(1, core, 0, 3)
                sending(SIBLING, 1, 0, 3).start()

        count = jobs_in(s)

        @pl.when(count > 0)
        def _():
            begin(job_at(AT_ONCE * s), 0)

        @pl.loop(0, AT_ONCE)
        def _(i):
            @pl.when(i + 1 < count)
            def _():
                begin(job_at(AT_ONCE * s + i + 1), (i + 1) % 2)

            @pl.when(i < count)
            def _():
                score(job_at(AT_ONCE * s + i), i % 2)

    for j in range(1, 4):
        taken = (blk + j) % 4
        pltpu.make_async_copy(ids.at[taken], ids.at[taken], got_i.at[taken]).wait()
    spots = out_ref.shape[1]
    example = lax.broadcasted_iota(jnp.int32, (spots, toks), 0)
    total = jnp.zeros((spots, 128), jnp.float32)
    for b in range(4):
        member = (ids[b, 0:1, :] == example).astype(jnp.float32)
        total += jnp.dot(
            member, sums[b // 2, (b % 2) * toks:(b % 2 + 1) * toks, :],
            precision=lax.Precision.HIGHEST, preferred_element_type=jnp.float32,
        )
    across_lanes = lax.dot_general(
        jnp.ones((8, 128), jnp.float32), total, (((1,), (1,)), ((), ())),
        precision=lax.Precision.HIGHEST, preferred_element_type=jnp.float32,
    )
    mine = lax.broadcasted_iota(jnp.int32, (8, spots), 0) == blk
    by_plane[z] = jnp.where(mine, across_lanes, 0.0)

    def shared(buffer, axis, me, phase):
        def sent(j):
            return pltpu.make_async_remote_copy(
                src_ref=buffer.at[me],
                dst_ref=buffer.at[me],
                send_sem=sent_s.at[phase, j - 1],
                recv_sem=got_s.at[phase, me],
                device_id={axis: (me + j) % 4},
                device_id_type=mesh_id,
            )

        for j in range(1, 4):
            sent(j).start()
        for j in range(1, 4):
            slot = (me + j) % 4
            pltpu.make_async_copy(buffer.at[slot], buffer.at[slot], got_s.at[phase, slot]).wait()
        result = (buffer[0] + buffer[1]) + (buffer[2] + buffer[3])
        for j in range(1, 4):
            sent(j).wait_send()
        return result

    by_block[blk] = shared(by_plane, "rows", z, 0)
    out_ref[...] = shared(by_block, "blk", blk, 1)

    for j in range(1, 4):
        ids_send(j).wait_send()
    for index in range(5):
        act_send(index, sibling, half, a_ref).wait_send()

    @pl.loop(0, QUARTERS)
    def _(u):
        slab_send(beside, PLANES, u).wait_send()

    @pl.loop(0, PLANES * QUARTERS)
    def _(i):
        m, q = i // QUARTERS, i % QUARTERS

        @pl.when(is_mid | (m < 3))
        def _():
            sending(SIBLING, 0, m, q).wait_send()
            sending(SIBLING, 1, m, q).wait_send()

        @pl.when(is_end)
        def _():
            @pl.when(m == 0)
            def _():
                sending(INNER, 0, m, q).wait_send()

                @pl.when(q == 3)
                def _():
                    sending(INNER, 1, m, q).wait_send()

            @pl.when((m == 0) | (m == 2) | ((m == 1) & (q == 3)))
            def _():
                sending(ACROSS, 0, m, q).wait_send()

        @pl.when(is_mid)
        def _():
            @pl.when(m < 2)
            def _():
                sending(INNER, 0, m, q).wait_send()

            @pl.when((m == 1) | (m == 2))
            def _():
                sending(OUTER, 0, m, q).wait_send()

            @pl.when(m == 1)
            def _():
                sending(INNER, 1, m, q).wait_send()

                @pl.when(q < 3)
                def _():
                    sending(OUTER, 1, m, q).wait_send()

            @pl.when((m == 1) | (m == 3) | ((m == 0) & (q < 3)))
            def _():
                sending(ACROSS, 0, m, q).wait_send()


def by_kernel(activations, out_grads, eigvecs, eigvals, segment_ids):
    toks, depth = activations.shape
    width = out_grads.shape[1]
    blocks = lax.axis_size("blk")
    number = eigvals.shape[0]
    examples = toks * blocks // SEG_MEAN
    spots = -(-examples // 128) * 128
    any_space = pl.BlockSpec(memory_space=pl.ANY)
    in_vmem = pl.BlockSpec(memory_space=pltpu.VMEM)
    scores, _ = pl.pallas_call(
        kernel,
        out_shape=(
            jax.ShapeDtypeStruct((8, spots), jnp.float32),
            jax.ShapeDtypeStruct((2, PLANES, 2 * toks, width), jnp.bfloat16),
        ),
        in_specs=[any_space] * 3 + [in_vmem],
        out_specs=(in_vmem, any_space),
        scratch_shapes=[
            pltpu.VMEM((PLANES + 1, depth, width), jnp.bfloat16),
            pltpu.VMEM((4, 2 * toks, depth), jnp.bfloat16),
            pltpu.VMEM((2, toks, width), jnp.bfloat16),
            pltpu.VMEM((2, 64, width), jnp.float32),
            pltpu.VMEM((2, 2 * toks, 128), jnp.float32),
            pltpu.VMEM((4, 8, toks), jnp.int32),
            pltpu.VMEM((4, 8, spots), jnp.float32),
            pltpu.VMEM((4, 8, spots), jnp.float32),
            pltpu.SemaphoreType.DMA((2, 2, PLANES, QUARTERS)),
            pltpu.SemaphoreType.DMA((4, 2, PLANES, QUARTERS)),
            pltpu.SemaphoreType.DMA((4, 2)),
            pltpu.SemaphoreType.DMA((5,)),
            pltpu.SemaphoreType.DMA((2, QUARTERS)),
            pltpu.SemaphoreType.DMA((QUARTERS,)),
            pltpu.SemaphoreType.DMA((4,)),
            pltpu.SemaphoreType.DMA((3,)),
            pltpu.SemaphoreType.DMA((2, 4)),
            pltpu.SemaphoreType.DMA((2, 3)),
            pltpu.SemaphoreType.DMA((6,)),
            pltpu.SemaphoreType.DMA((2,)),
        ],
        compiler_params=pltpu.CompilerParams(
            collective_id=0, has_side_effects=True, vmem_limit_bytes=60 * 2**20
        ),
        cost_estimate=pl.CostEstimate(
            flops=2 * blocks * toks * depth * width * PLANES,
            bytes_accessed=4 * depth * width * PLANES + 4 * blocks * toks * width * PLANES,
            transcendentals=0,
        ),
    )(activations, out_grads, eigvecs, jnp.broadcast_to(segment_ids[None, :], (8, toks)))
    return scores[:number, :examples].T / eigvals[None, :]


def local(activations, out_grads, eigvecs, eigvals, segment_ids):
    toks, depth = activations.shape
    fits = (
        lax.axis_size("blk") == 4
        and lax.axis_size("copies") == 2
        and eigvals.shape[0] == 4
        and lax.axis_size("rows") == PLANES
        and toks % (16 * QUARTERS) == 0
        and out_grads.shape[1] % 128 == 0
        and depth % 256 == 0
    )
    run = by_kernel if fits else by_ring
    return run(activations, out_grads, eigvecs, eigvals, segment_ids)


def solution(mesh):
    in_specs = (
        P(("copies", "blk"), "rows"),
        P(("copies", "blk"), "rows"),
        P("blk", "rows", None),
        P(),
        P(("copies", "blk")),
    )
    out_specs = P("copies", None)
    return jax.shard_map(local, mesh=mesh, in_specs=in_specs, out_specs=out_specs, check_vma=False)
```
